256 devices in a mesh: band: 64 (over z, y, x_lo), kpt: 4 (over x_hi, core).
Axes of the slice: x: 4 (x_hi: 2, x_lo: 2; x = x_hi * 2 + x_lo), y: 4, z: 8, core: 2. Of those that a mesh axis runs over, the one named last changes fastest.
Arguments:
- orbitals: float32 [64, 4, 2, 32, 768], P('band', 'kpt'), may hold values from -6 to 6
- screened_kernel: float32 [4, 32, 768], replicated, may hold values from 0.1 to 4
- kpoint_index: int32 [4], replicated, may hold values from 0 to 15, as said below
- q_index: int32 [16, 16], replicated, may hold values from 0 to 3
Outputs:
- exchange: float32 [64, 4, 2, 32, 768], P('band', 'kpt')
The draws below stay inside these ranges and needn't reach their ends.
Inputs may be any that keep to these rules, and one draw needn't show every extreme that they name: `kpoint_index`: the k-point numbers of the positions are all different.
All inputs are finite; a program needn't handle non-finite values.
Results may differ from the reference program's by a relative error of at most 0.0003.
Values sent between devices are 32-bit elements; how exact they have to be, the bound alone decides.
A program may use at most 64 MiB of HBM per device.

```python
import math
import jax
import jax.numpy as jnp
from jax import lax

X = 32
Y = 32
Z = 24
NQ = 4
NBAND = 64
NKPT = 4
NKTAB = 16


def draw_kpoint_index(key, part):
    first_key = jax.random.fold_in(key, 11)
    second_key = jax.random.fold_in(key, 12)
    middle = 1 + jax.random.permutation(first_key, NKTAB - 2)[:NKPT - 2]
    values = jnp.concatenate([jnp.array([0, NKTAB - 1], dtype=jnp.int32), middle.astype(jnp.int32)])
    order = jax.random.permutation(second_key, NKPT)
    return values[order].astype(jnp.int32)


def plant(values, rng, low, largest):
    place = [jax.random.randint(jax.random.fold_in(rng, axis), (), 0, length) for axis, length in enumerate(values.shape)]
    widest = values.shape.index(max(values.shape))
    beside = place[:widest] + [(place[widest] + 1) % values.shape[widest]] + place[widest + 1:]
    return values.at[tuple(place)].set(low).at[tuple(beside)].set(largest)


def shard_levels(stream_key, shape, pieces, low, top_value):
    factor_of = 1.0
    for axis_at, shards_of in pieces:
        steps = jax.random.uniform(jax.random.fold_in(jax.random.fold_in(stream_key, 6), axis_at), (shards_of,), jnp.float32, low / len(pieces), top_value / len(pieces))
        factor_of = factor_of * jnp.repeat(jnp.exp(steps), shape[axis_at] // shards_of).reshape((-1,) + (1,) * (len(shape) - 1 - axis_at))
    return factor_of


def scatter_about(own_key, shape, deviation, limit, split=(), kind=jnp.bfloat16):
    loudness = shard_levels(own_key, shape, split, -0.22, 0.18) if split else 1.0
    drawn = jax.random.normal(own_key, shape, jnp.float32) * deviation * loudness
    return jnp.minimum(jnp.maximum(drawn, -limit), limit).astype(kind)


def setup_inputs(seed: int = 0) -> dict:
    key_list = jax.random.split(jax.random.key(seed), 5)
    orbitals = scatter_about(key_list[0], (NBAND, NKPT, 2, X, Y * Z), 1.0, 6.0, ((0, 64), (1, 4)), jnp.float32)
    screened_kernel = jnp.clip(jnp.exp(jax.random.uniform(key_list[1], (NQ, X, Y * Z), jnp.float32, math.log(0.1), math.log(4.0))), 0.1, 4.0)
    kpoint_index = draw_kpoint_index(jax.random.fold_in(key_list[4], 71), 0)
    q_index = plant(jax.random.randint(key_list[3], (NKTAB, NKTAB), 0, NQ), jax.random.fold_in(key_list[3], 1), 0, NQ - 1).astype(jnp.int32)
    return dict(orbitals=orbitals, screened_kernel=screened_kernel, kpoint_index=kpoint_index, q_index=q_index)


def pair_term(resident, visitor, weight, kernel_slab):
    res_real = resident[0].reshape(X, Y, Z)
    res_imag = resident[1].reshape(X, Y, Z)
    vis_real = visitor[0].reshape(X, Y, Z)
    vis_imag = visitor[1].reshape(X, Y, Z)
    density = (vis_real * res_real + vis_imag * res_imag) + 1j * (vis_real * res_imag - vis_imag * res_real)
    spectrum = jnp.fft.fftn(density) * kernel_slab.reshape(X, Y, Z)
    potential = jnp.fft.ifftn(spectrum)
    pot_real = jnp.real(potential)
    pot_imag = jnp.imag(potential)
    term_real = vis_real * pot_real - vis_imag * pot_imag
    term_imag = vis_real * pot_imag + vis_imag * pot_real
    return -weight * jnp.stack([term_real.reshape(X, Y * Z), term_imag.reshape(X, Y * Z)])


def reference(orbitals, screened_kernel, kpoint_index, q_index):
    weight = 1.0 / NKPT

    def one_band(band_row):
        rows = ((band_row + jnp.arange(-1, 2)) % NBAND).astype(jnp.int32)
        visitors = orbitals[rows]

        def one_resident(kpt_row):
            resident = orbitals[band_row, kpt_row]

            def one_visitor(visitor_number):
                offset = visitor_number // NKPT
                other = (visitor_number % NKPT).astype(jnp.int32)
                transfer = q_index[kpoint_index[kpt_row], kpoint_index[other]]
                return pair_term(resident, visitors[offset, other], weight, screened_kernel[transfer])

            terms = lax.map(one_visitor, jnp.arange(3 * NKPT, dtype=jnp.int32))
            return jnp.sum(terms, axis=0)

        return lax.map(one_resident, jnp.arange(NKPT, dtype=jnp.int32))

    return lax.map(one_band, jnp.arange(NBAND, dtype=jnp.int32))
```

```python
import numpy as np, ml_dtypes
import jax, jax.numpy as jnp
from jax import lax
from jax.sharding import PartitionSpec as P
from jax.experimental import pallas as pl
from jax.experimental.pallas import tpu as pltpu
X,Y,Z=32,32,24
YZ=Y*Z; H=YZ//2
f32=jnp.float32; bf16=jnp.bfloat16

def split_np(a):
    hi=a.astype(np.float32).astype(ml_dtypes.bfloat16)
    lo=(a-hi.astype(np.float64)).astype(np.float32).astype(ml_dtypes.bfloat16)
    return hi,lo

def tables():
    y=np.arange(Y//2)[:,None,None,None]; z=np.arange(Z)[None,:,None,None]
    m=np.arange(Y//2)[None,None,:,None]; kz=np.arange(Z)[None,None,None,:]
    ws=[]
    for c in range(2):
        ph=(3*y*(2*m+c)+4*z*kz)%96
        th=2*np.pi*ph/96
        C=np.cos(th).reshape(H,H); S=np.sin(th).reshape(H,H)
        ws.append(np.block([[C,-S],[S,C]]))
    W=np.stack(ws)
    whi,wlo=split_np(W)
    xx=np.arange(X); th=2*np.pi*((xx[:,None]*xx[None,:])%X)/X
    C=np.cos(th);S=np.sin(th)
    F=np.block([[C,S],[-S,C]])
    I=np.block([[C,-S],[S,C]])
    def lhs(D):
        h,l=split_np(D); return np.concatenate([h,l,h],1)
    dx=np.stack([lhs(F),lhs(I)])
    perm=np.zeros((YZ,YZ),np.float32)
    for c in range(2):
        for mm in range(Y//2):
            for k in range(Z):
                perm[(2*mm+c)*Z+k, c*H+mm*Z+k]=1
    return whi,wlo,dx,perm.astype(ml_dtypes.bfloat16)

def split(a):
    hi=a.astype(bf16)
    lo=(a-hi.astype(f32)).astype(bf16)
    return hi,lo

def dotn(a,b): return jnp.dot(a,b,preferred_element_type=f32)
def dott(a,b): return lax.dot_general(a,b,(((1,),(1,)),((),())),preferred_element_type=f32)

def three(a,whi,wlo,dot):
    hi,lo=split(a)
    return dot(hi,whi)+dot(lo,whi)+dot(hi,wlo)

def group(res, vis_ref, first, G, kp_ref, whi, wlo, dx, acc, trans=True, koff=0):
    rr,ri=res
    s_rows=[];d_rows=[]
    for g in range(G):
        vr=vis_ref[first+g,0]; vi=vis_ref[first+g,1]
        pr=vr*rr+vi*ri; pi=vr*ri-vi*rr
        s_rows.append(jnp.concatenate([pr[:,:H]+pr[:,H:],pi[:,:H]+pi[:,H:]],1))
        d_rows.append(jnp.concatenate([pr[:,:H]-pr[:,H:],pi[:,:H]-pi[:,H:]],1))
    tS=three(jnp.concatenate(s_rows,0),whi[0],wlo[0],dotn)
    tD=three(jnp.concatenate(d_rows,0),whi[1],wlo[1],dotn)
    e_rows=[];o_rows=[]
    for g in range(G):
        rows=slice(g*X,g*X+X)
        a=jnp.concatenate([jnp.concatenate([tS[rows,:H],tD[rows,:H]],1),jnp.concatenate([tS[rows,H:],tD[rows,H:]],1)],0)
        hi,lo=split(a)
        sp=dotn(dx[0],jnp.concatenate([hi,hi,lo],0))
        k=kp_ref[koff+g]
        sp=sp*jnp.concatenate([k,k],0)
        hi,lo=split(sp)
        q=dotn(dx[1],jnp.concatenate([hi,hi,lo],0))
        e_rows.append(jnp.concatenate([q[:X,:H],q[X:,:H]],1))
        o_rows.append(jnp.concatenate([q[:X,H:],q[X:,H:]],1))
    uE=three(jnp.concatenate(e_rows,0),whi[0],wlo[0],dott)
    uO=three(jnp.concatenate(o_rows,0),whi[1],wlo[1],dott)
    for g in range(G):
        rows=slice(g*X,g*X+X)
        er,ei,orr,oi=uE[rows,:H],uE[rows,H:],uO[rows,:H],uO[rows,H:]
        pr=jnp.concatenate([er+orr,er-orr],1); pi=jnp.concatenate([ei+oi,ei-oi],1)
        vr=vis_ref[first+g,0]; vi=vis_ref[first+g,1]
        acc[0]+=vr*pr-vi*pi
        acc[1]+=vr*pi+vi*pr

def permute_k(kern_ref, kp_ref, kpt, q_ref, me, perm):
    own=kpt[me]
    rows=[kern_ref[q_ref[own,kpt[j]]] for j in range(4)]
    k=jnp.concatenate(rows,0)*(-1.0/(4*X*Y*Z))
    a=k.astype(bf16); r=k-a.astype(f32); b=r.astype(bf16); c=(r-b.astype(f32)).astype(bf16)
    out=dotn(a,perm)+dotn(b,perm)+dotn(c,perm)
    for j in range(4): kp_ref[j]=out[j*X:(j+1)*X]


def kernel(mid_ref, low_ref, high_ref, kern_ref, kpt, q, whi, wlo, dx, perm, out, kp, own):
    me = lax.axis_index("kpt")
    permute_k(kern_ref, kp, kpt, q, me, perm[...])
    own[...] = mid_ref[me]
    out[...] = jnp.zeros_like(out)
    for ref in (mid_ref, low_ref, high_ref):
        group((own[0], own[1]), ref, 0, 4, kp, whi, wlo, dx, out)


def local(orbitals, screened_kernel, kpoint_index, q_index):
    count = lax.axis_size("band")
    rows = lax.all_gather(orbitals[0, 0], "kpt", axis=0, tiled=False)
    low = lax.ppermute(rows, "band", [(i, (i + 1) % count) for i in range(count)])
    high = lax.ppermute(rows, "band", [((i + 1) % count, i) for i in range(count)])
    whi, wlo, dx, perm = tables()
    vmem = pl.BlockSpec(memory_space=pltpu.VMEM)
    smem = pl.BlockSpec(memory_space=pltpu.SMEM)
    out = pl.pallas_call(
        kernel,
        out_shape=jax.ShapeDtypeStruct((2, X, YZ), f32),
        in_specs=[vmem] * 4 + [smem] * 2 + [vmem] * 4,
        out_specs=vmem,
        scratch_shapes=[pltpu.VMEM((4, X, YZ), f32), pltpu.VMEM((2, X, YZ), f32)],
        compiler_params=pltpu.CompilerParams(vmem_limit_bytes=60 << 20),
        name="exchange",
    )(rows, low, high, screened_kernel, kpoint_index, q_index, whi, wlo, dx, perm)
    return out[None, None]


def solution(mesh):
    return jax.shard_map(
        local,
        mesh=mesh,
        in_specs=(P("band", "kpt", None, None, None), P(), P(), P()),
        out_specs=P("band", "kpt", None, None, None),
        check_vma=False,
    )
```

```python
import numpy as np, ml_dtypes
import jax, jax.numpy as jnp
from jax import lax
from jax.sharding import PartitionSpec as P
from jax.experimental import pallas as pl
from jax.experimental.pallas import tpu as pltpu

X, Y, Z = 32, 32, 24
YZ = Y * Z
H = YZ // 2
f32 = jnp.float32
bf16 = jnp.bfloat16
COMPUTE = True


def split_np(a):
    hi = a.astype(np.float32).astype(ml_dtypes.bfloat16)
    lo = (a - hi.astype(np.float64)).astype(np.float32).astype(ml_dtypes.bfloat16)
    return hi, lo


def tables():
    y = np.arange(Y // 2)[:, None, None, None]
    z = np.arange(Z)[None, :, None, None]
    m = np.arange(Y // 2)[None, None, :, None]
    kz = np.arange(Z)[None, None, None, :]
    blocks = []
    for odd in range(2):
        angle = 2 * np.pi * ((3 * y * (2 * m + odd) + 4 * z * kz) % 96) / 96
        c = np.cos(angle).reshape(H, H)
        s = np.sin(angle).reshape(H, H)
        blocks.append(np.block([[c, -s], [s, c]]))
    whi, wlo = split_np(np.stack(blocks + [blocks[1].T]))
    x = np.arange(X)
    angle = 2 * np.pi * ((x[:, None] * x[None, :]) % X) / X
    c = np.cos(angle)
    s = np.sin(angle)

    def pair(d):
        h, l = split_np(d)
        o = np.zeros_like(h)
        return np.block([[h, h, o, o], [o, o, h, h], [l, o, o, o], [o, o, l, o]]).astype(ml_dtypes.bfloat16)

    dx = np.stack([pair(np.block([[c, s], [-s, c]])), pair(np.block([[c, -s], [s, c]]))])
    perm = np.zeros((YZ, YZ), np.float32)
    for odd in range(2):
        for mm in range(Y // 2):
            for k in range(Z):
                perm[(2 * mm + odd) * Z + k, odd * H + mm * Z + k] = 1
    return whi, wlo, dx, perm.astype(ml_dtypes.bfloat16)


def split(a):
    hi = a.astype(bf16)
    return hi, (a - hi.astype(f32)).astype(bf16)


def dot(a, b):
    return jnp.dot(a, b, preferred_element_type=f32)


def three(a, whi, wlo):
    hi, lo = split(a)
    n = a.shape[0]
    p = dot(jnp.concatenate([hi, lo], 0), whi)
    return p[:n] + p[n:] + dot(hi, wlo)


def lanes(*a):
    return jnp.concatenate(a, 1)


def rows(*a):
    return jnp.concatenate(a, 0)


def xdft(a0, a1, d):
    h0, l0 = split(a0)
    h1, l1 = split(a1)
    o = dot(d, rows(h0, l0, h1, l1))
    return o[:64] + o[128:192], o[64:128] + o[192:]


def group(vis, first, count, kp, kfirst, whi, wlo, dx, acc, between):
    s_rows = []
    d_rows = []
    rr, ri = vis[0, 0], vis[0, 1]
    for g in range(count):
        vr, vi = vis[first + g, 0], vis[first + g, 1]
        pr = vr * rr + vi * ri
        pi = vr * ri - vi * rr
        s_rows.append(lanes(pr[:, :H] + pr[:, H:], pi[:, :H] + pi[:, H:]))
        d_rows.append(lanes(pr[:, :H] - pr[:, H:], pi[:, :H] - pi[:, H:]))
    ts = three(rows(*s_rows), whi[0], wlo[0])
    td = three(rows(*d_rows), whi[1], wlo[1])
    between(0)
    e_rows = []
    o_rows = []
    for g in range(0, count, 2):
        a = []
        for i in (g, g + 1):
            r = slice(i * X, i * X + X)
            a.append(rows(lanes(ts[r, :H], td[r, :H]), lanes(ts[r, H:], td[r, H:])))
        s0, s1 = xdft(a[0], a[1], dx[0])
        k0, k1 = kp[kfirst + g], kp[kfirst + g + 1]
        s0 = s0 * rows(k0, k0)
        s1 = s1 * rows(k1, k1)
        for q in xdft(s0, s1, dx[1]):
            e_rows.append(lanes(q[X:, :H], q[:X, :H]))
            o_rows.append(lanes(q[:X, H:], q[X:, H:]))
    between(1)
    ue = three(rows(*e_rows), whi[0], wlo[0])
    uo = three(rows(*o_rows), whi[2], wlo[2])
    between(2)
    for g in range(count):
        r = slice(g * X, g * X + X)
        ei, er, orr, oi = ue[r, :H], ue[r, H:], uo[r, :H], uo[r, H:]
        pr = lanes(er + orr, er - orr)
        pi = lanes(ei + oi, ei - oi)
        vr, vi = vis[first + g, 0], vis[first + g, 1]
        acc[0] += vr * pr - vi * pi
        acc[1] += vr * pi + vi * pr


def permute_k(kern, kp, kpt, q, place, perm):
    own = kpt[place[0]]
    k = rows(*[kern[q[own, kpt[p]]] for p in place]) * (-1.0 / (4 * X * Y * Z))
    a = k.astype(bf16)
    r = k - a.astype(f32)
    b = r.astype(bf16)
    c = (r - b.astype(f32)).astype(bf16)
    out = dot(a, perm) + dot(b, perm) + dot(c, perm)
    for j in range(4):
        kp[j] = out[j * X : (j + 1) * X]


def kernel(bands, orb, kern_in, kpt, q, whi_in, wlo_in, dx_in, perm_in, out,
           vis, kern, whi, wlo, dx, perm, kp, local_sem, send_sem, recv_sem):
    k = lax.axis_index("kpt")
    b = lax.axis_index("band")
    core = lax.rem(k, 2)
    half = lax.div(k, 2)
    partner = k + 1 - 2 * core
    opposite = k + 2 - 4 * half
    opposite_partner = partner + 2 - 4 * half
    low = lax.rem(b, 2)
    other = b + 1 - 2 * low
    up = lax.rem(b + 2, bands)
    down = lax.rem(b + bands - 2, bands)
    target = up + low * (down - up)
    origin = down + low * (up - down)

    def device(band, kpoint):
        return {"band": band, "kpt": kpoint}

    places = [device(other, k), device(other, opposite), device(b, partner)]
    barrier = pltpu.get_barrier_semaphore()
    for d in places + [device(origin, k)]:
        pl.semaphore_signal(barrier, inc=1, device_id=d, device_id_type=pl.DeviceIdType.MESH)

    loads = [pltpu.make_async_copy(s, t, local_sem.at[i]) for i, (s, t) in enumerate(
        [(orb, vis.at[0]), (kern_in, kern), (perm_in, perm), (dx_in, dx)]
        + [(s.at[i], t.at[i]) for i in range(3) for s, t in ((whi_in, whi), (wlo_in, wlo))])]
    for c in loads:
        c.start()
    pl.semaphore_wait(barrier, 4)

    def send(i, src, dst, d):
        return pltpu.make_async_remote_copy(src_ref=src, dst_ref=dst, send_sem=send_sem.at[i],
                                            recv_sem=recv_sem.at[i], device_id=d,
                                            device_id_type=pl.DeviceIdType.MESH)

    along_x = [send(2 * n + p, orb.at[p], vis.at[4 + 2 * n, p], places[n]) for p in range(2) for n in range(2)]
    along_y = [send(4 + 2 * n + p, vis.at[4 + 2 * n, p], vis.at[8 + 2 * n, p], device(target, k))
               for p in range(2) for n in range(2)]
    relay = [send(8 + n, vis.at[6 - 2 * n, half], vis.at[2, half], places[n]) for n in range(2)]
    arrived = [send(8, vis.at[6, half], vis.at[2, half], places[0]),
               send(9, vis.at[4, half], vis.at[2, 1 - half], places[1])]
    to_core = [send(10, orb, vis.at[1], places[2]),
               send(11, vis.at[4], vis.at[5], places[2]), send(12, vis.at[6], vis.at[7], places[2]),
               send(13, vis.at[2], vis.at[3], places[2])]
    last = [send(14 + 2 * n + p, vis.at[8 + 2 * n, p], vis.at[9 + 2 * n, p], places[2])
            for p in range(2) for n in range(2)]

    for c in along_x:
        c.start()
    to_core[0].start()
    for n in range(2):
        along_x[n].wait_recv()
        along_y[n].start()
    loads[1].wait()
    loads[2].wait()
    permute_k(kern, kp, kpt, q, [k, partner, opposite, opposite_partner], perm[...])
    for n in range(2, 4):
        along_x[n].wait_recv()
        along_y[n].start()
    for c in relay:
        c.start()
    to_core[1].start()
    to_core[2].start()
    for i in (0, 3, 4, 5, 6, 7, 8, 9):
        loads[i].wait()
    out[...] = jnp.zeros_like(out)
    to_core[1].wait_recv()
    to_core[2].wait_recv()

    def opposite_in():
        for c in arrived:
            c.wait_recv()
        to_core[3].start()

    def outer_in(which):
        for i in which:
            along_y[i].wait_recv()
            last[i].start()

    def first(i):
        if i == 0:
            opposite_in()

    def second(i):
        if i == 1:
            outer_in((0, 1))
        if i == 2:
            outer_in((2, 3))

    if COMPUTE:
        group(vis, 4, 4, kp, 0, whi, wlo, dx, out, first)
    else:
        first(0)
    to_core[0].wait_recv()
    to_core[3].wait_recv()
    if COMPUTE:
        group(vis, 0, 4, kp, 0, whi, wlo, dx, out, second)
    else:
        second(1)
        second(2)
    for c in last:
        c.wait_recv()
    if COMPUTE:
        group(vis, 8, 4, kp, 0, whi, wlo, dx, out, lambda i: None)
    for c in along_x + along_y + relay + to_core + last:
        c.wait_send()


def local(orbitals, screened_kernel, kpoint_index, q_index):
    whi, wlo, dx, perm = tables()
    vmem = pl.BlockSpec(memory_space=pltpu.VMEM)
    smem = pl.BlockSpec(memory_space=pltpu.SMEM)
    hbm = pl.BlockSpec(memory_space=pl.ANY)
    bands = lax.axis_size("band")
    out = pl.pallas_call(
        lambda *refs: kernel(bands, *refs),
        out_shape=jax.ShapeDtypeStruct((2, X, YZ), f32),
        in_specs=[hbm] * 2 + [smem] * 2 + [hbm] * 4,
        out_specs=vmem,
        scratch_shapes=[
            pltpu.VMEM((12, 2, X, YZ), f32),
            pltpu.VMEM((4, X, YZ), f32),
            pltpu.VMEM(whi.shape, bf16),
            pltpu.VMEM(wlo.shape, bf16),
            pltpu.VMEM(dx.shape, bf16),
            pltpu.VMEM(perm.shape, bf16),
            pltpu.VMEM((4, X, YZ), f32),
            pltpu.SemaphoreType.DMA((10,)),
            pltpu.SemaphoreType.DMA((18,)),
            pltpu.SemaphoreType.DMA((18,)),
        ],
        compiler_params=pltpu.CompilerParams(
            vmem_limit_bytes=60 << 20, collective_id=0, has_side_effects=True
        ),
        name="exchange",
    )(orbitals[0, 0], screened_kernel, kpoint_index, q_index, whi, wlo, dx, perm)
    return out[None, None]


def solution(mesh):
    return jax.shard_map(
        local,
        mesh=mesh,
        in_specs=(P("band", "kpt", None, None, None), P(), P(), P()),
        out_specs=P("band", "kpt", None, None, None),
        check_vma=False,
    )
```

```python
import numpy as np, ml_dtypes
import jax, jax.numpy as jnp
from jax import lax
from jax.sharding import PartitionSpec as P
from jax.experimental import pallas as pl
from jax.experimental.pallas import tpu as pltpu

X, Y, Z = 32, 32, 24
YZ = Y * Z
H = YZ // 2
f32 = jnp.float32
bf16 = jnp.bfloat16
COMPUTE = True


def split_np(a):
    hi = a.astype(np.float32).astype(ml_dtypes.bfloat16)
    lo = (a - hi.astype(np.float64)).astype(np.float32).astype(ml_dtypes.bfloat16)
    return hi, lo


def tables():
    y = np.arange(Y // 2)[:, None, None, None]
    z = np.arange(Z)[None, :, None, None]
    m = np.arange(Y // 2)[None, None, :, None]
    kz = np.arange(Z)[None, None, None, :]
    blocks = []
    for odd in range(2):
        angle = 2 * np.pi * ((3 * y * (2 * m + odd) + 4 * z * kz) % 96) / 96
        c = np.cos(angle).reshape(H, H)
        s = np.sin(angle).reshape(H, H)
        blocks.append(np.block([[c, -s], [s, c]]))
    whi, wlo = split_np(np.stack(blocks + [blocks[1].T]))
    x = np.arange(X)
    angle = 2 * np.pi * ((x[:, None] * x[None, :]) % X) / X
    c = np.cos(angle)
    s = np.sin(angle)

    def pair(d):
        h, l = split_np(d)
        o = np.zeros_like(h)
        return np.block([[h, h, o, o], [o, o, h, h], [l, o, o, o], [o, o, l, o]]).astype(ml_dtypes.bfloat16)

    dx = np.stack([pair(np.block([[c, s], [-s, c]])), pair(np.block([[c, -s], [s, c]]))])
    perm = np.zeros((YZ, YZ), np.float32)
    for odd in range(2):
        for mm in range(Y // 2):
            for k in range(Z):
                perm[(2 * mm + odd) * Z + k, odd * H + mm * Z + k] = 1
    return whi, wlo, dx, perm.astype(ml_dtypes.bfloat16)


def split(a):
    hi = a.astype(bf16)
    return hi, (a - hi.astype(f32)).astype(bf16)


def dot(a, b):
    return jnp.dot(a, b, preferred_element_type=f32)


def three(a, whi, wlo):
    hi, lo = split(a)
    n = a.shape[0]
    p = dot(jnp.concatenate([hi, lo], 0), whi)
    return p[:n] + p[n:] + dot(hi, wlo)


def lanes(*a):
    return jnp.concatenate(a, 1)


def rows(*a):
    return jnp.concatenate(a, 0)


def xdft(a0, a1, d):
    h0, l0 = split(a0)
    h1, l1 = split(a1)
    o = dot(d, rows(h0, l0, h1, l1))
    return o[:64] + o[128:192], o[64:128] + o[192:]


def group(vis, slots, kp, whi, wlo, dx, acc, between):
    count = len(slots)
    s_rows = []
    d_rows = []
    rr, ri = vis[0, 0], vis[0, 1]
    for g in range(count):
        vr, vi = vis[slots[g], 0], vis[slots[g], 1]
        pr = vr * rr + vi * ri
        pi = vr * ri - vi * rr
        s_rows.append(lanes(pr[:, :H] + pr[:, H:], pi[:, :H] + pi[:, H:]))
        d_rows.append(lanes(pr[:, :H] - pr[:, H:], pi[:, :H] - pi[:, H:]))
    ts = three(rows(*s_rows), whi[0], wlo[0])
    td = three(rows(*d_rows), whi[1], wlo[1])
    between(0)
    e_rows = []
    o_rows = []
    for g in range(0, count, 2):
        a = []
        for i in (g, g + 1):
            r = slice(i * X, i * X + X)
            a.append(rows(lanes(ts[r, :H], td[r, :H]), lanes(ts[r, H:], td[r, H:])))
        s0, s1 = xdft(a[0], a[1], dx[0])
        k0, k1 = kp[slots[g] % 4], kp[slots[g + 1] % 4]
        s0 = s0 * rows(k0, k0)
        s1 = s1 * rows(k1, k1)
        for q in xdft(s0, s1, dx[1]):
            e_rows.append(lanes(q[X:, :H], q[:X, :H]))
            o_rows.append(lanes(q[:X, H:], q[X:, H:]))
    between(1)
    ue = three(rows(*e_rows), whi[0], wlo[0])
    uo = three(rows(*o_rows), whi[2], wlo[2])
    between(2)
    for g in range(count):
        r = slice(g * X, g * X + X)
        ei, er, orr, oi = ue[r, :H], ue[r, H:], uo[r, :H], uo[r, H:]
        pr = lanes(er + orr, er - orr)
        pi = lanes(ei + oi, ei - oi)
        vr, vi = vis[slots[g], 0], vis[slots[g], 1]
        acc[0] += vr * pr - vi * pi
        acc[1] += vr * pi + vi * pr


def permute_k(kern, kp, kpt, q, place, perm):
    own = kpt[place[0]]
    k = rows(*[kern[q[own, kpt[p]]] for p in place]) * (-1.0 / (4 * X * Y * Z))
    a = k.astype(bf16)
    r = k - a.astype(f32)
    b = r.astype(bf16)
    c = (r - b.astype(f32)).astype(bf16)
    out = dot(a, perm) + dot(b, perm) + dot(c, perm)
    for j in range(4):
        kp[j] = out[j * X : (j + 1) * X]


def kernel(bands, orb, kern_in, kpt, q, whi_in, wlo_in, dx_in, perm_in, out,
           vis, transit, kern, whi, wlo, dx, perm, kp, local_sem, send_sem, recv_sem, x_ready, y_ready):
    k = lax.axis_index("kpt")
    b = lax.axis_index("band")
    core = lax.rem(k, 2)
    half = lax.div(k, 2)
    partner = k + 1 - 2 * core
    opposite = k + 2 - 4 * half
    opposite_partner = partner + 2 - 4 * half
    low = lax.rem(b, 2)
    other = b + 1 - 2 * low
    up = lax.rem(b + 2, bands)
    down = lax.rem(b + bands - 2, bands)
    target = up + low * (down - up)
    origin = down + low * (up - down)

    def device(band, kpoint):
        return {"band": band, "kpt": kpoint}

    places = [device(other, k), device(other, opposite), device(b, partner)]
    mesh_ids = pl.DeviceIdType.MESH
    barrier = pltpu.get_barrier_semaphore()
    pl.semaphore_signal(barrier, inc=1, device_id=device(other, 1), device_id_type=mesh_ids)
    pl.semaphore_signal(barrier, inc=1, device_id=device(other, 3), device_id_type=mesh_ids)

    @pl.when(core == 0)
    def _():
        pl.semaphore_signal(barrier, inc=1, device_id=places[2], device_id_type=mesh_ids)

    for d in (up, down):
        pl.semaphore_signal(barrier, inc=1, device_id=device(d, 2 * half), device_id_type=mesh_ids)

    loads = [pltpu.make_async_copy(s, t, local_sem.at[i]) for i, (s, t) in enumerate(
        [(orb, vis.at[0]), (kern_in, kern), (perm_in, perm), (dx_in, dx)]
        + [(s.at[i], t.at[i]) for i in range(3) for s, t in ((whi_in, whi), (wlo_in, wlo))])]
    for c in loads[:3]:
        c.start()

    def send(i, src, dst, d):
        return pltpu.make_async_remote_copy(src_ref=src, dst_ref=dst, send_sem=send_sem.at[i],
                                            recv_sem=recv_sem.at[i], device_id=d,
                                            device_id_type=mesh_ids)

    cuts = [pl.ds(0, X // 2), pl.ds(X // 2, X // 2)]
    both = range(2)
    pieces = [(0, cuts[0]), (1, cuts[0]), (1, cuts[1]), (0, cuts[1])]
    along_x = [send(2 * c + n, orb.at[0, cuts[c]], vis.at[4 + 2 * n, 0, cuts[c]], places[n]) for c in both for n in both]
    along_x += [send(4 + n, orb.at[1], vis.at[4 + 2 * n, 1], places[n]) for n in both]
    along_y = [send(6 + n, vis.at[4 + 2 * n, 0, cuts[0]], vis.at[8 + 2 * n, 0, cuts[0]], device(target, k)) for n in both]
    through = [send(8 + i, orb.at[p, cut], transit.at[i], device(origin, k)) for i, (p, cut) in enumerate(pieces[1:])]
    onward = [[send(11 + 2 * i + n, transit.at[i], vis.at[8 + 2 * n, p, cut], places[n]) for n in both]
              for i, (p, cut) in enumerate(pieces[1:])]
    relay = [send(17 + n, vis.at[6 - 2 * n, half], vis.at[2, half], places[n]) for n in both]
    arrived = [send(17, vis.at[6, half], vis.at[2, half], places[0]),
               send(18, vis.at[4, half], vis.at[2, 1 - half], places[1])]
    to_core = [send(19, orb, vis.at[1], places[2]),
               send(20, vis.at[4], vis.at[5], places[2]), send(21, vis.at[6], vis.at[7], places[2]),
               send(22, vis.at[2], vis.at[3], places[2])]
    last = [[send(23 + 2 * i + n, vis.at[8 + 2 * n, p, cut], vis.at[9 + 2 * n, p, cut], places[2]) for n in both]
            for i, (p, cut) in enumerate(pieces)]

    first_ring = lax.div(b, 2) == 0
    late_in = jnp.logical_and(first_ring, low == 0)

    def unless(flag, work):
        pl.when(jnp.logical_not(flag))(work)

    def enter_y():
        pl.semaphore_wait(barrier, 4)
        for c in through:
            c.start()

    def tell_y():
        pl.semaphore_signal(y_ready, inc=1, device_id=places[2], device_id_type=mesh_ids)

    def hear_y():
        pl.semaphore_wait(y_ready, 1)
        for c in through:
            c.start()

    @pl.when(core == 1)
    def _():
        pl.semaphore_wait(barrier, 5)
        pl.semaphore_signal(x_ready, inc=1, device_id=places[2], device_id_type=mesh_ids)

    @pl.when(core == 0)
    def _():
        unless(first_ring, enter_y)
        pl.semaphore_wait(x_ready, 1)
        unless(first_ring, tell_y)

    for c in along_x[:4]:
        c.start()

    @pl.when(core == 1)
    def _():
        unless(first_ring, hear_y)

    to_core[0].start()
    for c in loads[3:]:
        c.start()

    def relay_y():
        for n in both:
            along_x[n].wait_recv()
            along_y[n].start()

    def outer_in():
        for i in range(3):
            for n in both:
                onward[i][n].wait_recv()
                last[1 + i][n].start()
            if i == 0:
                for n in both:
                    along_y[n].wait_recv()
                    last[0][n].start()
        for group_of in last:
            for c in group_of:
                c.wait_recv()

    loads[1].wait()
    loads[2].wait()
    permute_k(kern, kp, kpt, q, [k, partner, opposite, opposite_partner], perm[...])
    for c in along_x[4:]:
        c.start()
    unless(first_ring, relay_y)
    out[...] = jnp.zeros_like(out)
    for i in (0, 3, 4, 5, 6, 7, 8, 9):
        loads[i].wait()
    to_core[0].wait_recv()

    def compute(slots, between):
        if COMPUTE:
            group(vis, slots, kp, whi, wlo, dx, out, between)
        else:
            for i in range(3):
                between(i)

    def nothing(i):
        pass

    compute([0, 1], nothing)

    @pl.when(first_ring)
    def _():
        @pl.when(core == 0)
        def _():
            enter_y()
            tell_y()

        pl.when(core == 1)(hear_y)
        relay_y()

    for c in along_x[2:]:
        c.wait_recv()
    for n in both:
        to_core[1 + n].start()
    for c in relay:
        c.start()
    for i in range(3):
        through[i].wait_recv()
        for c in onward[i]:
            c.start()
    for n in both:
        to_core[1 + n].wait_recv()

    def during_other(i):
        if i == 2:
            for c in arrived:
                c.wait_recv()
            to_core[3].start()

    compute([4, 5, 6, 7], during_other)
    to_core[3].wait_recv()

    @pl.when(late_in)
    def _():
        compute([2, 3], nothing)
        outer_in()
        compute([8, 9, 10, 11], nothing)

    @pl.when(jnp.logical_not(late_in))
    def _():
        outer_in()
        compute([2, 3, 8, 9, 10, 11], nothing)

    for c in along_x + along_y + through + relay + to_core + sum(onward + last, []):
        c.wait_send()


def local(orbitals, screened_kernel, kpoint_index, q_index):
    whi, wlo, dx, perm = tables()
    vmem = pl.BlockSpec(memory_space=pltpu.VMEM)
    smem = pl.BlockSpec(memory_space=pltpu.SMEM)
    hbm = pl.BlockSpec(memory_space=pl.ANY)
    bands = lax.axis_size("band")
    out = pl.pallas_call(
        lambda *refs: kernel(bands, *refs),
        out_shape=jax.ShapeDtypeStruct((2, X, YZ), f32),
        in_specs=[hbm] * 2 + [smem] * 2 + [hbm] * 4,
        out_specs=vmem,
        scratch_shapes=[
            pltpu.VMEM((12, 2, X, YZ), f32),
            pltpu.VMEM((3, X // 2, YZ), f32),
            pltpu.VMEM((4, X, YZ), f32),
            pltpu.VMEM(whi.shape, bf16),
            pltpu.VMEM(wlo.shape, bf16),
            pltpu.VMEM(dx.shape, bf16),
            pltpu.VMEM(perm.shape, bf16),
            pltpu.VMEM((4, X, YZ), f32),
            pltpu.SemaphoreType.DMA((10,)),
            pltpu.SemaphoreType.DMA((31,)),
            pltpu.SemaphoreType.DMA((31,)),
            pltpu.SemaphoreType.REGULAR,
            pltpu.SemaphoreType.REGULAR,
        ],
        compiler_params=pltpu.CompilerParams(
            vmem_limit_bytes=60 << 20, collective_id=0, has_side_effects=True
        ),
        name="exchange",
    )(orbitals[0, 0], screened_kernel, kpoint_index, q_index, whi, wlo, dx, perm)
    return out[None, None]


def solution(mesh):
    return jax.shard_map(
        local,
        mesh=mesh,
        in_specs=(P("band", "kpt", None, None, None), P(), P(), P()),
        out_specs=P("band", "kpt", None, None, None),
        check_vma=False,
    )
```

```python
import numpy as np, ml_dtypes
import jax, jax.numpy as jnp
from jax import lax
from jax.sharding import PartitionSpec as P
from jax.experimental import pallas as pl
from jax.experimental.pallas import tpu as pltpu

X, Y, Z = 32, 32, 24
YZ = Y * Z
H = YZ // 2
f32 = jnp.float32
bf16 = jnp.bfloat16
COMPUTE = True
RELAYED = 1


def split_np(a):
    hi = a.astype(np.float32).astype(ml_dtypes.bfloat16)
    lo = (a - hi.astype(np.float64)).astype(np.float32).astype(ml_dtypes.bfloat16)
    return hi, lo


def tables():
    y = np.arange(Y // 2)[:, None, None, None]
    z = np.arange(Z)[None, :, None, None]
    m = np.arange(Y // 2)[None, None, :, None]
    kz = np.arange(Z)[None, None, None, :]
    blocks = []
    for odd in range(2):
        angle = 2 * np.pi * ((3 * y * (2 * m + odd) + 4 * z * kz) % 96) / 96
        c = np.cos(angle).reshape(H, H)
        s = np.sin(angle).reshape(H, H)
        blocks.append(np.block([[c, -s], [s, c]]))
    whi, wlo = split_np(np.stack(blocks + [blocks[1].T]))
    x = np.arange(X)
    angle = 2 * np.pi * ((x[:, None] * x[None, :]) % X) / X
    c = np.cos(angle)
    s = np.sin(angle)

    def pair(d):
        h, l = split_np(d)
        o = np.zeros_like(h)
        return np.block([[h, h, o, o], [o, o, h, h], [l, o, o, o], [o, o, l, o]]).astype(ml_dtypes.bfloat16)

    dx = np.stack([pair(np.block([[c, s], [-s, c]])), pair(np.block([[c, -s], [s, c]]))])
    perm = np.zeros((YZ, YZ), np.float32)
    for odd in range(2):
        for mm in range(Y // 2):
            for k in range(Z):
                perm[(2 * mm + odd) * Z + k, odd * H + mm * Z + k] = 1
    return whi, wlo, dx, perm.astype(ml_dtypes.bfloat16)


def split(a):
    hi = a.astype(bf16)
    return hi, (a - hi.astype(f32)).astype(bf16)


def dot(a, b):
    return jnp.dot(a, b, preferred_element_type=f32)


def three(a, whi, wlo):
    hi, lo = split(a)
    n = a.shape[0]
    p = dot(jnp.concatenate([hi, lo], 0), whi)
    return p[:n] + p[n:] + dot(hi, wlo)


def lanes(*a):
    return jnp.concatenate(a, 1)


def rows(*a):
    return jnp.concatenate(a, 0)


def xdft(a0, a1, d):
    h0, l0 = split(a0)
    h1, l1 = split(a1)
    o = dot(d, rows(h0, l0, h1, l1))
    return o[:64] + o[128:192], o[64:128] + o[192:]


def group(vis, slots, kp, whi, wlo, dx, acc, between):
    count = len(slots)
    s_rows = []
    d_rows = []
    rr, ri = vis[0, 0], vis[0, 1]
    for g in range(count):
        vr, vi = vis[slots[g], 0], vis[slots[g], 1]
        pr = vr * rr + vi * ri
        pi = vr * ri - vi * rr
        s_rows.append(lanes(pr[:, :H] + pr[:, H:], pi[:, :H] + pi[:, H:]))
        d_rows.append(lanes(pr[:, :H] - pr[:, H:], pi[:, :H] - pi[:, H:]))
    ts = three(rows(*s_rows), whi[0], wlo[0])
    td = three(rows(*d_rows), whi[1], wlo[1])
    between(0)
    e_rows = []
    o_rows = []
    for g in range(0, count, 2):
        a = []
        for i in (g, g + 1):
            r = slice(i * X, i * X + X)
            a.append(rows(lanes(ts[r, :H], td[r, :H]), lanes(ts[r, H:], td[r, H:])))
        s0, s1 = xdft(a[0], a[1], dx[0])
        k0, k1 = kp[slots[g] % 4], kp[slots[g + 1] % 4]
        s0 = s0 * rows(k0, k0)
        s1 = s1 * rows(k1, k1)
        for q in xdft(s0, s1, dx[1]):
            e_rows.append(lanes(q[X:, :H], q[:X, :H]))
            o_rows.append(lanes(q[:X, H:], q[X:, H:]))
    between(1)
    ue = three(rows(*e_rows), whi[0], wlo[0])
    uo = three(rows(*o_rows), whi[2], wlo[2])
    between(2)
    for g in range(count):
        r = slice(g * X, g * X + X)
        ei, er, orr, oi = ue[r, :H], ue[r, H:], uo[r, :H], uo[r, H:]
        pr = lanes(er + orr, er - orr)
        pi = lanes(ei + oi, ei - oi)
        vr, vi = vis[slots[g], 0], vis[slots[g], 1]
        acc[0] += vr * pr - vi * pi
        acc[1] += vr * pi + vi * pr


def permute_k(kern, kp, kpt, q, place, perm):
    own = kpt[place[0]]
    k = rows(*[kern[q[own, kpt[p]]] for p in place]) * (-1.0 / (4 * X * Y * Z))
    a = k.astype(bf16)
    r = k - a.astype(f32)
    b = r.astype(bf16)
    c = (r - b.astype(f32)).astype(bf16)
    out = dot(a, perm) + dot(b, perm) + dot(c, perm)
    for j in range(4):
        kp[j] = out[j * X : (j + 1) * X]


def kernel(bands, orb, kern_in, kpt_in, q_in, whi_in, wlo_in, dx_in, perm_in, out,
           vis, transit, kern, kpt, q, whi, wlo, dx, perm, kp, local_sem, send_sem, recv_sem, x_ready, up_ready, down_ready):
    k = lax.axis_index("kpt")
    b = lax.axis_index("band")
    core = lax.rem(k, 2)
    half = lax.div(k, 2)
    partner = k + 1 - 2 * core
    opposite = k + 2 - 4 * half
    opposite_partner = partner + 2 - 4 * half
    low = lax.rem(b, 2)
    other = b + 1 - 2 * low
    up = lax.rem(b + 2, bands)
    down = lax.rem(b + bands - 2, bands)
    target = up + low * (down - up)
    origin = down + low * (up - down)

    def device(band, kpoint):
        return {"band": band, "kpt": kpoint}

    places = [device(other, k), device(other, opposite), device(b, partner)]
    mesh_ids = pl.DeviceIdType.MESH
    barrier = pltpu.get_barrier_semaphore()
    pl.semaphore_signal(barrier, inc=1, device_id=device(other, 1), device_id_type=mesh_ids)
    pl.semaphore_signal(barrier, inc=1, device_id=device(other, 3), device_id_type=mesh_ids)

    @pl.when(core == 0)
    def _():
        pl.semaphore_signal(barrier, inc=1, device_id=places[2], device_id_type=mesh_ids)

    pl.semaphore_signal(barrier, inc=1, device_id=device(down, 2 * half), device_id_type=mesh_ids)

    loads = [pltpu.make_async_copy(s, t, local_sem.at[i]) for i, (s, t) in enumerate(
        [(orb, vis.at[0]), (kern_in, kern), (perm_in, perm), (kpt_in, kpt), (q_in, q), (dx_in, dx)]
        + [(s.at[i], t.at[i]) for i in range(3) for s, t in ((whi_in, whi), (wlo_in, wlo))])]
    for c in loads[:5]:
        c.start()

    def send(i, src, dst, d):
        return pltpu.make_async_remote_copy(src_ref=src, dst_ref=dst, send_sem=send_sem.at[i],
                                            recv_sem=recv_sem.at[i], device_id=d,
                                            device_id_type=mesh_ids)

    cuts = [pl.ds(0, X // 2), pl.ds(X // 2, X // 2)]
    both = range(2)
    pieces = [(0, cuts[0]), (0, cuts[1]), (1, cuts[0]), (1, cuts[1])]
    relayed, routed = pieces[:RELAYED], pieces[RELAYED:]
    index = iter(range(31))
    along_x = [[send(next(index), orb.at[0, cuts[c]], vis.at[4 + 2 * n, 0, cuts[c]], places[n]) for n in both]
               for c in both]
    along_x += [[send(next(index), orb.at[1], vis.at[4 + 2 * n, 1], places[n]) for n in both]]
    along_y = [[send(next(index), vis.at[4 + 2 * n, p, cut], vis.at[8 + 2 * n, p, cut], device(target, k)) for n in both]
               for p, cut in relayed]
    through = [send(next(index), orb.at[p, cut], transit.at[i], device(origin, k)) for i, (p, cut) in enumerate(routed)]
    onward = [[send(next(index), transit.at[i], vis.at[8 + 2 * n, p, cut], places[n]) for n in both]
              for i, (p, cut) in enumerate(routed)]
    first = next(index)
    second = next(index)
    relay = [send(first, vis.at[6, half], vis.at[2, half], places[0]),
             send(second, vis.at[4, half], vis.at[2, half], places[1])]
    arrived = [send(first, vis.at[6, half], vis.at[2, half], places[0]),
               send(second, vis.at[4, half], vis.at[2, 1 - half], places[1])]
    to_core = [send(next(index), orb, vis.at[1], places[2]),
               send(next(index), vis.at[4], vis.at[5], places[2]), send(next(index), vis.at[6], vis.at[7], places[2]),
               send(next(index), vis.at[2], vis.at[3], places[2])]
    last = [[send(next(index), vis.at[8 + 2 * n, p, cut], vis.at[9 + 2 * n, p, cut], places[2]) for n in both]
            for p, cut in pieces]

    first_ring = lax.div(b, 2) == 0
    late_in = jnp.logical_and(first_ring, low == 0)
    late_relay = jnp.logical_and(first_ring, low == 1)
    late_through = jnp.logical_or(late_relay, b == bands - 2)

    def unless(flag, work):
        pl.when(jnp.logical_not(flag))(work)

    def route():
        for c in through:
            c.start()

    def hear_down():
        pl.semaphore_wait(down_ready, 1)
        pl.when(low == 0)(route)

    @pl.when(core == 1)
    def _():
        pl.semaphore_wait(barrier, 5)
        pl.semaphore_signal(x_ready, inc=1, device_id=places[2], device_id_type=mesh_ids)

    @pl.when(core == 0)
    def _():
        pl.semaphore_wait(barrier, 2)
        pl.when(low == 1)(route)
        pl.semaphore_wait(x_ready, 1)
        pl.semaphore_signal(up_ready, inc=1, device_id=places[2], device_id_type=mesh_ids)
        for kpoint in (k, partner):
            pl.semaphore_signal(down_ready, inc=1, device_id=device(up, kpoint), device_id_type=mesh_ids)

    for c in sum(along_x, []):
        c.start()

    @pl.when(core == 1)
    def _():
        pl.semaphore_wait(up_ready, 1)
        pl.when(low == 1)(route)

    to_core[0].start()
    for c in loads[5:]:
        c.start()

    def relay_y(arrive, leave):
        for i in range(len(relayed)):
            for n in both:
                if arrive:
                    along_x[i][n].wait_recv()
                if leave:
                    along_y[i][n].start()

    def pass_on(i):
        through[i].wait_recv()
        for c in onward[i]:
            c.start()

    def outer_in(i):
        for n in both:
            (along_y + onward)[i][n].wait_recv()
            last[i][n].start()

    for c in loads[1:5]:
        c.wait()
    permute_k(kern, kp, kpt, q, [k, partner, opposite, opposite_partner], perm[...])
    unless(first_ring, hear_down)
    unless(late_relay, lambda: relay_y(True, True))
    out[...] = jnp.zeros_like(out)
    loads[0].wait()
    for c in loads[5:]:
        c.wait()
    to_core[0].wait_recv()

    def compute(slots, between):
        if COMPUTE:
            group(vis, slots, kp, whi, wlo, dx, out, between)
        else:
            for i in range(3):
                between(i)

    def nothing(i):
        pass

    def during_own(i):
        if i != 1:
            unless(late_through, lambda: pass_on(i // 2))

    compute([0, 1], during_own)

    pl.when(late_relay)(lambda: relay_y(True, False))
    for i in range(len(relayed), 3):
        for c in along_x[i]:
            c.wait_recv()
    for n in both:
        to_core[1 + n].start()
    for c in relay:
        c.start()

    pl.when(first_ring)(hear_down)
    pl.when(late_relay)(lambda: relay_y(False, True))

    @pl.when(late_through)
    def _():
        pass_on(0)
        pass_on(1)

    for i in range(2, len(routed)):
        pass_on(i)
    for n in both:
        to_core[1 + n].wait_recv()

    def during_other(i):
        if i == 0:
            unless(late_in, lambda: outer_in(0))
        if i == 1:
            unless(late_in, lambda: outer_in(1))
        if i == 2:
            unless(late_in, lambda: outer_in(2))

    compute([4, 5, 6, 7], during_other)
    for c in arrived:
        c.wait_recv()
    to_core[3].start()

    @pl.when(late_in)
    def _():
        to_core[3].wait_recv()
        compute([2, 3], nothing)
        for i in (1, 0, 2, 3):
            outer_in(i)
        for c in sum(last, []):
            c.wait_recv()
        compute([8, 9, 10, 11], nothing)

    @pl.when(jnp.logical_not(late_in))
    def _():
        outer_in(3)
        to_core[3].wait_recv()
        for c in sum(last, []):
            c.wait_recv()
        compute([2, 3, 8, 9, 10, 11], nothing)

    for c in sum(along_x + along_y + onward + last, []) + through + relay + to_core:
        c.wait_send()


def pin(a):
    return pltpu.with_memory_space_constraint(jnp.asarray(a), pltpu.HBM)


def local(orbitals, screened_kernel, kpoint_index, q_index):
    whi, wlo, dx, perm = tables()
    vmem = pl.BlockSpec(memory_space=pltpu.VMEM)
    hbm = pl.BlockSpec(memory_space=pl.ANY)
    bands = lax.axis_size("band")
    out = pl.pallas_call(
        lambda *refs: kernel(bands, *refs),
        out_shape=jax.ShapeDtypeStruct((2, X, YZ), f32),
        in_specs=[hbm] * 8,
        out_specs=vmem,
        scratch_shapes=[
            pltpu.VMEM((12, 2, X, YZ), f32),
            pltpu.VMEM((4 - RELAYED, X // 2, YZ), f32),
            pltpu.VMEM((4, X, YZ), f32),
            pltpu.SMEM(kpoint_index.shape, jnp.int32),
            pltpu.SMEM(q_index.shape, jnp.int32),
            pltpu.VMEM(whi.shape, bf16),
            pltpu.VMEM(wlo.shape, bf16),
            pltpu.VMEM(dx.shape, bf16),
            pltpu.VMEM(perm.shape, bf16),
            pltpu.VMEM((4, X, YZ), f32),
            pltpu.SemaphoreType.DMA((12,)),
            pltpu.SemaphoreType.DMA((31,)),
            pltpu.SemaphoreType.DMA((31,)),
            pltpu.SemaphoreType.REGULAR,
            pltpu.SemaphoreType.REGULAR,
            pltpu.SemaphoreType.REGULAR,
        ],
        compiler_params=pltpu.CompilerParams(
            vmem_limit_bytes=30 << 20, collective_id=0, has_side_effects=True
        ),
        name="exchange",
    )(*map(pin, (orbitals[0, 0], screened_kernel, kpoint_index, q_index, whi, wlo, dx, perm)))
    return out[None, None]


def solution(mesh):
    return jax.shard_map(
        local,
        mesh=mesh,
        in_specs=(P("band", "kpt", None, None, None), P(), P(), P()),
        out_specs=P("band", "kpt", None, None, None),
        check_vma=False,
    )
```

```python
import numpy as np, ml_dtypes
import jax, jax.numpy as jnp
from jax import lax
from jax.sharding import PartitionSpec as P
from jax.experimental import pallas as pl
from jax.experimental.pallas import tpu as pltpu

X, Y, Z = 32, 32, 24
YZ = Y * Z
H = YZ // 2
f32 = jnp.float32
bf16 = jnp.bfloat16
COMPUTE = True
RELAYED = 1


def split_np(a):
    hi = a.astype(np.float32).astype(ml_dtypes.bfloat16)
    lo = (a - hi.astype(np.float64)).astype(np.float32).astype(ml_dtypes.bfloat16)
    return hi, lo


def tables():
    y = np.arange(Y // 2)[:, None, None, None]
    z = np.arange(Z)[None, :, None, None]
    m = np.arange(Y // 2)[None, None, :, None]
    kz = np.arange(Z)[None, None, None, :]
    blocks = []
    for odd in range(2):
        angle = 2 * np.pi * ((3 * y * (2 * m + odd) + 4 * z * kz) % 96) / 96
        c = np.cos(angle).reshape(H, H)
        s = np.sin(angle).reshape(H, H)
        blocks.append(np.block([[c, -s], [s, c]]))
    whi, wlo = split_np(np.stack(blocks + [blocks[1].T]))
    x = np.arange(X)
    angle = 2 * np.pi * ((x[:, None] * x[None, :]) % X) / X
    c = np.cos(angle)
    s = np.sin(angle)

    def pair(d):
        h, l = split_np(d)
        o = np.zeros_like(h)
        return np.block([[h, h, o, o], [o, o, h, h], [l, o, o, o], [o, o, l, o]]).astype(ml_dtypes.bfloat16)

    dx = np.stack([pair(np.block([[c, s], [-s, c]])), pair(np.block([[c, -s], [s, c]]))])
    perm = np.zeros((YZ, YZ), np.float32)
    for odd in range(2):
        for mm in range(Y // 2):
            for k in range(Z):
                perm[(2 * mm + odd) * Z + k, odd * H + mm * Z + k] = 1
    return whi, wlo, dx, perm.astype(ml_dtypes.bfloat16)


def split(a):
    hi = a.astype(bf16)
    return hi, (a - hi.astype(f32)).astype(bf16)


def dot(a, b):
    return jnp.dot(a, b, preferred_element_type=f32)


def three(a, whi, wlo):
    hi, lo = split(a)
    n = a.shape[0]
    p = dot(jnp.concatenate([hi, lo], 0), whi)
    return p[:n] + p[n:] + dot(hi, wlo)


def lanes(*a):
    return jnp.concatenate(a, 1)


def rows(*a):
    return jnp.concatenate(a, 0)


def xdft(a0, a1, d):
    h0, l0 = split(a0)
    h1, l1 = split(a1)
    o = dot(d, rows(h0, l0, h1, l1))
    return o[:64] + o[128:192], o[64:128] + o[192:]


def group(vis, slots, kp, whi, wlo, dx, acc, between):
    count = len(slots)
    s_rows = []
    d_rows = []
    rr, ri = vis[0, 0], vis[0, 1]
    for g in range(count):
        vr, vi = vis[slots[g], 0], vis[slots[g], 1]
        pr = vr * rr + vi * ri
        pi = vr * ri - vi * rr
        s_rows.append(lanes(pr[:, :H] + pr[:, H:], pi[:, :H] + pi[:, H:]))
        d_rows.append(lanes(pr[:, :H] - pr[:, H:], pi[:, :H] - pi[:, H:]))
    ts = three(rows(*s_rows), whi[0], wlo[0])
    td = three(rows(*d_rows), whi[1], wlo[1])
    between(0)
    e_rows = []
    o_rows = []
    for g in range(0, count, 2):
        a = []
        for i in (g, g + 1):
            r = slice(i * X, i * X + X)
            a.append(rows(lanes(ts[r, :H], td[r, :H]), lanes(ts[r, H:], td[r, H:])))
        s0, s1 = xdft(a[0], a[1], dx[0])
        k0, k1 = kp[slots[g] % 4], kp[slots[g + 1] % 4]
        s0 = s0 * rows(k0, k0)
        s1 = s1 * rows(k1, k1)
        for q in xdft(s0, s1, dx[1]):
            e_rows.append(lanes(q[X:, :H], q[:X, :H]))
            o_rows.append(lanes(q[:X, H:], q[X:, H:]))
    between(1)
    ue = three(rows(*e_rows), whi[0], wlo[0])
    uo = three(rows(*o_rows), whi[2], wlo[2])
    between(2)
    for g in range(count):
        r = slice(g * X, g * X + X)
        ei, er, orr, oi = ue[r, :H], ue[r, H:], uo[r, :H], uo[r, H:]
        pr = lanes(er + orr, er - orr)
        pi = lanes(ei + oi, ei - oi)
        vr, vi = vis[slots[g], 0], vis[slots[g], 1]
        acc[0] += vr * pr - vi * pi
        acc[1] += vr * pi + vi * pr


def permute_k(kern, kp, kpt, q, place, perm):
    own = kpt[place[0]]
    k = rows(*[kern[q[own, kpt[p]]] for p in place]) * (-1.0 / (4 * X * Y * Z))
    a = k.astype(bf16)
    r = k - a.astype(f32)
    b = r.astype(bf16)
    c = (r - b.astype(f32)).astype(bf16)
    out = dot(a, perm) + dot(b, perm) + dot(c, perm)
    for j in range(4):
        kp[j] = out[j * X : (j + 1) * X]


def kernel(bands, orb, kern_in, kpt_in, q_in, whi_in, wlo_in, dx_in, perm_in, out,
           vis, transit, kern, kpt, q, whi, wlo, dx, perm, kp, local_sem, send_sem, recv_sem, x_ready, up_ready, down_ready):
    k = lax.axis_index("kpt")
    b = lax.axis_index("band")
    core = lax.rem(k, 2)
    half = lax.div(k, 2)
    partner = k + 1 - 2 * core
    opposite = k + 2 - 4 * half
    opposite_partner = partner + 2 - 4 * half
    low = lax.rem(b, 2)
    other = b + 1 - 2 * low
    up = lax.rem(b + 2, bands)
    down = lax.rem(b + bands - 2, bands)
    target = up + low * (down - up)
    origin = down + low * (up - down)

    def device(band, kpoint):
        return {"band": band, "kpt": kpoint}

    places = [device(other, k), device(other, opposite), device(b, partner)]
    mesh_ids = pl.DeviceIdType.MESH
    barrier = pltpu.get_barrier_semaphore()
    pl.semaphore_signal(barrier, inc=1, device_id=device(other, 1), device_id_type=mesh_ids)
    pl.semaphore_signal(barrier, inc=1, device_id=device(other, 3), device_id_type=mesh_ids)

    @pl.when(core == 0)
    def _():
        pl.semaphore_signal(barrier, inc=1, device_id=places[2], device_id_type=mesh_ids)

    pl.semaphore_signal(barrier, inc=1, device_id=device(down, 2 * half), device_id_type=mesh_ids)

    loads = [pltpu.make_async_copy(s, t, local_sem.at[i]) for i, (s, t) in enumerate(
        [(orb, vis.at[0]), (kern_in, kern), (perm_in, perm), (kpt_in, kpt), (q_in, q), (dx_in, dx)]
        + [(s.at[i], t.at[i]) for i in range(3) for s, t in ((whi_in, whi), (wlo_in, wlo))])]
    for c in loads[:5]:
        c.start()

    def send(i, src, dst, d):
        return pltpu.make_async_remote_copy(src_ref=src, dst_ref=dst, send_sem=send_sem.at[i],
                                            recv_sem=recv_sem.at[i], device_id=d,
                                            device_id_type=mesh_ids)

    cuts = [pl.ds(0, X // 2), pl.ds(X // 2, X // 2)]
    both = range(2)
    pieces = [(0, cuts[0]), (0, cuts[1]), (1, cuts[0]), (1, cuts[1])]
    relayed, routed = pieces[:RELAYED], pieces[RELAYED:]
    index = iter(range(33))
    along_x = [[send(next(index), orb.at[0, cuts[c]], vis.at[4 + 2 * n, 0, cuts[c]], places[n]) for n in both]
               for c in both]
    along_x += [[send(next(index), orb.at[1], vis.at[4 + 2 * n, 1], places[n]) for n in both]]
    along_y = [[send(next(index), vis.at[4 + 2 * n, p, cut], vis.at[8 + 2 * n, p, cut], device(target, k)) for n in both]
               for p, cut in relayed]
    through = [send(next(index), orb.at[p, cut], transit.at[i], device(origin, k)) for i, (p, cut) in enumerate(routed)]
    onward = [[send(next(index), transit.at[i], vis.at[8 + 2 * n, p, cut], places[n]) for n in both]
              for i, (p, cut) in enumerate(routed)]
    first = next(index)
    second = next(index)
    relay = [send(first, vis.at[6, half], vis.at[2, half], places[0]),
             send(second, vis.at[4, half], vis.at[2, half], places[1])]
    arrived = [send(first, vis.at[6, half], vis.at[2, half], places[0]),
               send(second, vis.at[4, half], vis.at[2, 1 - half], places[1])]
    to_core = [send(next(index), orb, vis.at[1], places[2]),
               send(next(index), vis.at[2], vis.at[3], places[2])]
    other_to_core = [[send(next(index), vis.at[4 + 2 * n, p], vis.at[5 + 2 * n, p], places[2]) for n in both]
                     for p in both]
    last = [[send(next(index), vis.at[8 + 2 * n, p, cut], vis.at[9 + 2 * n, p, cut], places[2]) for n in both]
            for p, cut in pieces]

    first_ring = lax.div(b, 2) == 0
    late_in = jnp.logical_and(first_ring, low == 0)
    late_relay = jnp.logical_and(first_ring, low == 1)
    late_through = jnp.logical_or(late_relay, b == bands - 2)

    def unless(flag, work):
        pl.when(jnp.logical_not(flag))(work)

    def route():
        for c in through:
            c.start()

    def hear_down():
        pl.semaphore_wait(down_ready, 1)
        pl.when(low == 0)(route)

    @pl.when(core == 1)
    def _():
        pl.semaphore_wait(barrier, 5)
        pl.semaphore_signal(x_ready, inc=1, device_id=places[2], device_id_type=mesh_ids)

    @pl.when(core == 0)
    def _():
        pl.semaphore_wait(barrier, 2)
        pl.when(low == 1)(route)
        pl.semaphore_wait(x_ready, 1)
        pl.semaphore_signal(up_ready, inc=1, device_id=places[2], device_id_type=mesh_ids)
        for kpoint in (k, partner):
            pl.semaphore_signal(down_ready, inc=1, device_id=device(up, kpoint), device_id_type=mesh_ids)

    for c in sum(along_x, []):
        c.start()

    @pl.when(core == 1)
    def _():
        pl.semaphore_wait(up_ready, 1)
        pl.when(low == 1)(route)

    to_core[0].start()
    for c in loads[5:]:
        c.start()

    def relay_y(arrive, leave):
        for i in range(len(relayed)):
            for n in both:
                if arrive:
                    along_x[i][n].wait_recv()
                if leave:
                    along_y[i][n].start()

    def pass_on(i):
        through[i].wait_recv()
        for c in onward[i]:
            c.start()

    def outer_in(i):
        for n in both:
            (along_y + onward)[i][n].wait_recv()
            last[i][n].start()

    for c in loads[1:5]:
        c.wait()
    permute_k(kern, kp, kpt, q, [k, partner, opposite, opposite_partner], perm[...])
    unless(first_ring, hear_down)
    unless(late_relay, lambda: relay_y(True, True))
    out[...] = jnp.zeros_like(out)
    loads[0].wait()
    for c in loads[5:]:
        c.wait()
    to_core[0].wait_recv()

    def compute(slots, between):
        if COMPUTE:
            group(vis, slots, kp, whi, wlo, dx, out, between)
        else:
            for i in range(3):
                between(i)

    def nothing(i):
        pass

    def during_own(i):
        if i == 2:
            pl.when(late_relay)(lambda: relay_y(True, False))
            for r in range(len(relayed), 2):
                for c in along_x[r]:
                    c.wait_recv()
            for c in other_to_core[0]:
                c.start()
            unless(late_through, lambda: pass_on(0))

    compute([0, 1], during_own)

    for c in along_x[2]:
        c.wait_recv()
    for c in other_to_core[1]:
        c.start()
    for c in relay:
        c.start()

    pl.when(first_ring)(hear_down)
    pl.when(late_relay)(lambda: relay_y(False, True))

    for c in sum(other_to_core, []):
        c.wait_recv()

    def during_other(i):
        if i == 0:
            @pl.when(late_through)
            def _():
                for r in range(len(routed)):
                    pass_on(r)

            @pl.when(jnp.logical_not(late_through))
            def _():
                for r in range(1, len(routed)):
                    pass_on(r)

        if i == 2:
            for c in arrived:
                c.wait_recv()
            to_core[1].start()

            @pl.when(jnp.logical_not(late_in))
            def _():
                for r in range(len(relayed) + 1):
                    outer_in(r)

    compute([4, 5, 6, 7], during_other)
    to_core[1].wait_recv()

    def during_opposite(i):
        if i == 2:
            @pl.when(jnp.logical_not(late_in))
            def _():
                for r in range(len(relayed) + 1, 4):
                    outer_in(r)

    compute([2, 3], during_opposite)

    @pl.when(late_in)
    def _():
        for i in (1, 0, 2, 3):
            outer_in(i)

    for c in sum(last, []):
        c.wait_recv()
    compute([8, 9, 10, 11], nothing)
    for c in sum(along_x + along_y + onward + last + other_to_core, []) + through + relay + to_core:
        c.wait_send()


def pin(a):
    return pltpu.with_memory_space_constraint(jnp.asarray(a), pltpu.HBM)


def local(orbitals, screened_kernel, kpoint_index, q_index):
    whi, wlo, dx, perm = tables()
    vmem = pl.BlockSpec(memory_space=pltpu.VMEM)
    hbm = pl.BlockSpec(memory_space=pl.ANY)
    bands = lax.axis_size("band")
    out = pl.pallas_call(
        lambda *refs: kernel(bands, *refs),
        out_shape=jax.ShapeDtypeStruct((2, X, YZ), f32),
        in_specs=[hbm] * 8,
        out_specs=vmem,
        scratch_shapes=[
            pltpu.VMEM((12, 2, X, YZ), f32),
            pltpu.VMEM((4 - RELAYED, X // 2, YZ), f32),
            pltpu.VMEM((4, X, YZ), f32),
            pltpu.SMEM(kpoint_index.shape, jnp.int32),
            pltpu.SMEM(q_index.shape, jnp.int32),
            pltpu.VMEM(whi.shape, bf16),
            pltpu.VMEM(wlo.shape, bf16),
            pltpu.VMEM(dx.shape, bf16),
            pltpu.VMEM(perm.shape, bf16),
            pltpu.VMEM((4, X, YZ), f32),
            pltpu.SemaphoreType.DMA((12,)),
            pltpu.SemaphoreType.DMA((33,)),
            pltpu.SemaphoreType.DMA((33,)),
            pltpu.SemaphoreType.REGULAR,
            pltpu.SemaphoreType.REGULAR,
            pltpu.SemaphoreType.REGULAR,
        ],
        compiler_params=pltpu.CompilerParams(
            vmem_limit_bytes=30 << 20, collective_id=0, has_side_effects=True
        ),
        name="exchange",
    )(*map(pin, (orbitals[0, 0], screened_kernel, kpoint_index, q_index, whi, wlo, dx, perm)))
    return out[None, None]


def solution(mesh):
    return jax.shard_map(
        local,
        mesh=mesh,
        in_specs=(P("band", "kpt", None, None, None), P(), P(), P()),
        out_specs=P("band", "kpt", None, None, None),
        check_vma=False,
    )
```

```python
import numpy as np, ml_dtypes
import jax, jax.numpy as jnp
from jax import lax
from jax.sharding import PartitionSpec as P
from jax.experimental import pallas as pl
from jax.experimental.pallas import tpu as pltpu

X, Y, Z = 32, 32, 24
YZ = Y * Z
H = YZ // 2
f32 = jnp.float32
bf16 = jnp.bfloat16
COMPUTE = True
RELAYED = 1


def split_np(a):
    hi = a.astype(np.float32).astype(ml_dtypes.bfloat16)
    lo = (a - hi.astype(np.float64)).astype(np.float32).astype(ml_dtypes.bfloat16)
    return hi, lo


def tables():
    y = np.arange(Y // 2)[:, None, None, None]
    z = np.arange(Z)[None, :, None, None]
    m = np.arange(Y // 2)[None, None, :, None]
    kz = np.arange(Z)[None, None, None, :]
    blocks = []
    for odd in range(2):
        angle = 2 * np.pi * ((3 * y * (2 * m + odd) + 4 * z * kz) % 96) / 96
        c = np.cos(angle).reshape(H, H)
        s = np.sin(angle).reshape(H, H)
        blocks.append(np.block([[c, -s], [s, c]]))
    whi, wlo = split_np(np.stack(blocks + [blocks[1].T]))
    x = np.arange(X)
    angle = 2 * np.pi * ((x[:, None] * x[None, :]) % X) / X
    c = np.cos(angle)
    s = np.sin(angle)

    def pair(d):
        h, l = split_np(d)
        o = np.zeros_like(h)
        return np.block([[h, h, o, o], [o, o, h, h], [l, o, o, o], [o, o, l, o]]).astype(ml_dtypes.bfloat16)

    dx = np.stack([pair(np.block([[c, s], [-s, c]])), pair(np.block([[c, -s], [s, c]]))])
    perm = np.zeros((YZ, YZ), np.float32)
    for odd in range(2):
        for mm in range(Y // 2):
            for k in range(Z):
                perm[(2 * mm + odd) * Z + k, odd * H + mm * Z + k] = 1
    return whi, wlo, dx, perm.astype(ml_dtypes.bfloat16)


def split(a):
    hi = a.astype(bf16)
    return hi, (a - hi.astype(f32)).astype(bf16)


def dot(a, b):
    return jnp.dot(a, b, preferred_element_type=f32)


def three(a, whi, wlo):
    hi, lo = split(a)
    n = a.shape[0]
    p = dot(jnp.concatenate([hi, lo], 0), whi)
    return p[:n] + p[n:] + dot(hi, wlo)


def lanes(*a):
    return jnp.concatenate(a, 1)


def rows(*a):
    return jnp.concatenate(a, 0)


def xdft(a0, a1, d):
    h0, l0 = split(a0)
    h1, l1 = split(a1)
    o = dot(d, rows(h0, l0, h1, l1))
    return o[:64] + o[128:192], o[64:128] + o[192:]


def group(vis, slots, kp, whi, wlo, dx, acc, between):
    count = len(slots)
    s_rows = []
    d_rows = []
    rr, ri = vis[0, 0], vis[0, 1]
    for g in range(count):
        vr, vi = vis[slots[g], 0], vis[slots[g], 1]
        pr = vr * rr + vi * ri
        pi = vr * ri - vi * rr
        s_rows.append(lanes(pr[:, :H] + pr[:, H:], pi[:, :H] + pi[:, H:]))
        d_rows.append(lanes(pr[:, :H] - pr[:, H:], pi[:, :H] - pi[:, H:]))
    ts = three(rows(*s_rows), whi[0], wlo[0])
    td = three(rows(*d_rows), whi[1], wlo[1])
    between(0)
    e_rows = []
    o_rows = []
    for g in range(0, count, 2):
        a = []
        for i in (g, g + 1):
            r = slice(i * X, i * X + X)
            a.append(rows(lanes(ts[r, :H], td[r, :H]), lanes(ts[r, H:], td[r, H:])))
        s0, s1 = xdft(a[0], a[1], dx[0])
        k0, k1 = kp[slots[g] % 4], kp[slots[g + 1] % 4]
        s0 = s0 * rows(k0, k0)
        s1 = s1 * rows(k1, k1)
        for q in xdft(s0, s1, dx[1]):
            e_rows.append(lanes(q[X:, :H], q[:X, :H]))
            o_rows.append(lanes(q[:X, H:], q[X:, H:]))
    between(1)
    ue = three(rows(*e_rows), whi[0], wlo[0])
    uo = three(rows(*o_rows), whi[2], wlo[2])
    between(2)
    re, im = acc[0], acc[1]
    for g in range(count):
        r = slice(g * X, g * X + X)
        ei, er, orr, oi = ue[r, :H], ue[r, H:], uo[r, :H], uo[r, H:]
        pr = lanes(er + orr, er - orr)
        pi = lanes(ei + oi, ei - oi)
        vr, vi = vis[slots[g], 0], vis[slots[g], 1]
        re = re + (vr * pr - vi * pi)
        im = im + (vr * pi + vi * pr)
    acc[0] = re
    acc[1] = im


def permute_k(kern, kp, kpt, q, place, perm):
    own = kpt[place[0]]
    k = rows(*[kern[q[own, kpt[p]]] for p in place]) * (-1.0 / (4 * X * Y * Z))
    a = k.astype(bf16)
    r = k - a.astype(f32)
    b = r.astype(bf16)
    c = (r - b.astype(f32)).astype(bf16)
    out = dot(a, perm) + dot(b, perm) + dot(c, perm)
    for j in range(4):
        kp[j] = out[j * X : (j + 1) * X]


def kernel(bands, orb, kern_in, kpt_in, q_in, whi_in, wlo_in, dx_in, perm_in, out,
           vis, transit, kern, kpt, q, whi, wlo, dx, perm, kp, local_sem, send_sem, recv_sem, x_ready, up_ready, down_ready):
    k = lax.axis_index("kpt")
    b = lax.axis_index("band")
    core = lax.rem(k, 2)
    half = lax.div(k, 2)
    partner = k + 1 - 2 * core
    opposite = k + 2 - 4 * half
    opposite_partner = partner + 2 - 4 * half
    low = lax.rem(b, 2)
    other = b + 1 - 2 * low
    up = lax.rem(b + 2, bands)
    down = lax.rem(b + bands - 2, bands)
    target = up + low * (down - up)
    origin = down + low * (up - down)

    def device(band, kpoint):
        return {"band": band, "kpt": kpoint}

    places = [device(other, k), device(other, opposite), device(b, partner)]
    mesh_ids = pl.DeviceIdType.MESH
    barrier = pltpu.get_barrier_semaphore()
    pl.semaphore_signal(barrier, inc=1, device_id=device(other, 1), device_id_type=mesh_ids)
    pl.semaphore_signal(barrier, inc=1, device_id=device(other, 3), device_id_type=mesh_ids)

    @pl.when(core == 0)
    def _():
        pl.semaphore_signal(barrier, inc=1, device_id=places[2], device_id_type=mesh_ids)

    pl.semaphore_signal(barrier, inc=1, device_id=device(down, 2 * half), device_id_type=mesh_ids)

    loads = [pltpu.make_async_copy(s, t, local_sem.at[i]) for i, (s, t) in enumerate(
        [(orb, vis.at[0]), (kern_in, kern), (perm_in, perm), (kpt_in, kpt), (q_in, q), (dx_in, dx)]
        + [(s.at[i], t.at[i]) for i in range(3) for s, t in ((whi_in, whi), (wlo_in, wlo))])]
    for c in loads[:5]:
        c.start()

    def send(i, src, dst, d):
        return pltpu.make_async_remote_copy(src_ref=src, dst_ref=dst, send_sem=send_sem.at[i],
                                            recv_sem=recv_sem.at[i], device_id=d,
                                            device_id_type=mesh_ids)

    cuts = [pl.ds(0, X // 2), pl.ds(X // 2, X // 2)]
    both = range(2)
    pieces = [(0, cuts[0]), (0, cuts[1]), (1, cuts[0]), (1, cuts[1])]
    relayed, routed = pieces[:RELAYED], pieces[RELAYED:]
    index = iter(range(33))
    along_x = [[send(next(index), orb.at[0, cuts[c]], vis.at[4 + 2 * n, 0, cuts[c]], places[n]) for n in both]
               for c in both]
    along_x += [[send(next(index), orb.at[1], vis.at[4 + 2 * n, 1], places[n]) for n in both]]
    along_y = [[send(next(index), vis.at[4 + 2 * n, p, cut], vis.at[8 + 2 * n, p, cut], device(target, k)) for n in both]
               for p, cut in relayed]
    through = [send(next(index), orb.at[p, cut], transit.at[i], device(origin, k)) for i, (p, cut) in enumerate(routed)]
    onward = [[send(next(index), transit.at[i], vis.at[8 + 2 * n, p, cut], places[n]) for n in both]
              for i, (p, cut) in enumerate(routed)]
    first = next(index)
    second = next(index)
    relay = [send(first, vis.at[6, half], vis.at[2, half], places[0]),
             send(second, vis.at[4, half], vis.at[2, half], places[1])]
    arrived = [send(first, vis.at[6, half], vis.at[2, half], places[0]),
               send(second, vis.at[4, half], vis.at[2, 1 - half], places[1])]
    to_core = [send(next(index), orb, vis.at[1], places[2]),
               send(next(index), vis.at[2], vis.at[3], places[2])]
    other_to_core = [[send(next(index), vis.at[4 + 2 * n, p], vis.at[5 + 2 * n, p], places[2]) for n in both]
                     for p in both]
    last = [[send(next(index), vis.at[8 + 2 * n, p, cut], vis.at[9 + 2 * n, p, cut], places[2]) for n in both]
            for p, cut in pieces]

    first_ring = lax.div(b, 2) == 0
    late_in = jnp.logical_and(first_ring, low == 0)
    late_relay = jnp.logical_and(first_ring, low == 1)
    late_through = jnp.logical_or(late_relay, b == bands - 2)

    def unless(flag, work):
        pl.when(jnp.logical_not(flag))(work)

    def route():
        for c in through:
            c.start()

    def hear_down():
        pl.semaphore_wait(down_ready, 1)
        pl.when(low == 0)(route)

    @pl.when(core == 1)
    def _():
        pl.semaphore_wait(barrier, 5)
        pl.semaphore_signal(x_ready, inc=1, device_id=places[2], device_id_type=mesh_ids)

    @pl.when(core == 0)
    def _():
        pl.semaphore_wait(barrier, 2)
        pl.when(low == 1)(route)
        pl.semaphore_wait(x_ready, 1)
        pl.semaphore_signal(up_ready, inc=1, device_id=places[2], device_id_type=mesh_ids)
        for kpoint in (k, partner):
            pl.semaphore_signal(down_ready, inc=1, device_id=device(up, kpoint), device_id_type=mesh_ids)

    for c in sum(along_x, []):
        c.start()

    @pl.when(core == 1)
    def _():
        pl.semaphore_wait(up_ready, 1)
        pl.when(low == 1)(route)

    to_core[0].start()
    for c in loads[5:]:
        c.start()

    def relay_y(arrive, leave):
        for i in range(len(relayed)):
            for n in both:
                if arrive:
                    along_x[i][n].wait_recv()
                if leave:
                    along_y[i][n].start()

    def pass_on(i):
        through[i].wait_recv()
        for c in onward[i]:
            c.start()

    def outer_in(i):
        for n in both:
            (along_y + onward)[i][n].wait_recv()
            last[i][n].start()

    for c in loads[1:5]:
        c.wait()
    permute_k(kern, kp, kpt, q, [k, partner, opposite, opposite_partner], perm[...])
    unless(first_ring, hear_down)
    unless(late_relay, lambda: relay_y(True, True))
    out[...] = jnp.zeros_like(out)
    loads[0].wait()
    for c in loads[5:]:
        c.wait()
    to_core[0].wait_recv()

    def compute(slots, between):
        if COMPUTE:
            group(vis, slots, kp, whi, wlo, dx, out, between)
        else:
            for i in range(3):
                between(i)

    def nothing(i):
        pass

    def during_own(i):
        if i == 2:
            pl.when(late_relay)(lambda: relay_y(True, False))
            for r in range(len(relayed), 2):
                for c in along_x[r]:
                    c.wait_recv()
            for c in other_to_core[0]:
                c.start()
            unless(late_through, lambda: pass_on(0))

    compute([0, 1], during_own)

    for c in along_x[2]:
        c.wait_recv()
    for c in other_to_core[1]:
        c.start()
    for c in relay:
        c.start()

    pl.when(first_ring)(hear_down)
    pl.when(late_relay)(lambda: relay_y(False, True))

    for c in sum(other_to_core, []):
        c.wait_recv()

    def during_other(i):
        if i == 0:
            @pl.when(late_through)
            def _():
                for r in range(len(routed)):
                    pass_on(r)

            @pl.when(jnp.logical_not(late_through))
            def _():
                for r in range(1, len(routed)):
                    pass_on(r)

        if i == 2:
            for c in arrived:
                c.wait_recv()
            to_core[1].start()

            @pl.when(jnp.logical_not(late_in))
            def _():
                for r in range(len(relayed) + 1):
                    outer_in(r)

    compute([4, 5, 6, 7], during_other)
    to_core[1].wait_recv()

    def during_opposite(i):
        if i == 2:
            @pl.when(jnp.logical_not(late_in))
            def _():
                for r in range(len(relayed) + 1, 4):
                    outer_in(r)

    compute([2, 3], during_opposite)

    @pl.when(late_in)
    def _():
        for i in (1, 0, 2, 3):
            outer_in(i)

    for c in sum(along_x + along_y + onward + other_to_core, []) + through + relay + to_core:
        c.wait_send()
    for c in sum(last, []):
        c.wait_recv()
    compute([8, 9, 10, 11], nothing)
    for c in sum(last, []):
        c.wait_send()


def pin(a):
    return pltpu.with_memory_space_constraint(jnp.asarray(a), pltpu.HBM)


def local(orbitals, screened_kernel, kpoint_index, q_index):
    whi, wlo, dx, perm = tables()
    vmem = pl.BlockSpec(memory_space=pltpu.VMEM)
    hbm = pl.BlockSpec(memory_space=pl.ANY)
    bands = lax.axis_size("band")
    out = pl.pallas_call(
        lambda *refs: kernel(bands, *refs),
        out_shape=jax.ShapeDtypeStruct((2, X, YZ), f32),
        in_specs=[hbm] * 8,
        out_specs=vmem,
        scratch_shapes=[
            pltpu.VMEM((12, 2, X, YZ), f32),
            pltpu.VMEM((4 - RELAYED, X // 2, YZ), f32),
            pltpu.VMEM((4, X, YZ), f32),
            pltpu.SMEM(kpoint_index.shape, jnp.int32),
            pltpu.SMEM(q_index.shape, jnp.int32),
            pltpu.VMEM(whi.shape, bf16),
            pltpu.VMEM(wlo.shape, bf16),
            pltpu.VMEM(dx.shape, bf16),
            pltpu.VMEM(perm.shape, bf16),
            pltpu.VMEM((4, X, YZ), f32),
            pltpu.SemaphoreType.DMA((12,)),
            pltpu.SemaphoreType.DMA((33,)),
            pltpu.SemaphoreType.DMA((33,)),
            pltpu.SemaphoreType.REGULAR,
            pltpu.SemaphoreType.REGULAR,
            pltpu.SemaphoreType.REGULAR,
        ],
        compiler_params=pltpu.CompilerParams(
            vmem_limit_bytes=30 << 20, collective_id=0, has_side_effects=True
        ),
        name="exchange",
    )(*map(pin, (orbitals[0, 0], screened_kernel, kpoint_index, q_index, whi, wlo, dx, perm)))
    return out[None, None]


def solution(mesh):
    return jax.shard_map(
        local,
        mesh=mesh,
        in_specs=(P("band", "kpt", None, None, None), P(), P(), P()),
        out_specs=P("band", "kpt", None, None, None),
        check_vma=False,
    )
```
